32 devices in a mesh: seq: 16 (over z, y, x), head: 2 (over core).
Axes of the slice: x: 2, y: 2, z: 4, core: 2. Of those that a mesh axis runs over, the one named last changes fastest.
Arguments:
- query_in: bfloat16 [4096, 4096], P('seq', 'head'), may hold values from -1200 to 1200
- key_in: bfloat16 [4096, 4096], P('seq', 'head'), may hold values from -1200 to 1200
- value_in: bfloat16 [4096, 4096], P('seq', 'head'), may hold values from -6 to 6
- out_grad: bfloat16 [4096, 4096], P('seq', 'head'), may hold values from -6 to 6
- query_gain: float32 [4096], P('head'), may hold values from 0.5 to 2
- key_gain: float32 [4096], P('head'), may hold values from 0.5 to 2
- random_blocks: int32 [64, 3], replicated, may hold values from 0 to 63, as said below
- global_blocks: int32 [2], replicated, may hold values from 0 to 63, as said below
Outputs:
- attn_out: bfloat16 [4096, 4096], P('seq', 'head')
- query_grad: bfloat16 [4096, 4096], P('seq', 'head')
- key_grad: bfloat16 [4096, 4096], P('seq', 'head')
- value_grad: bfloat16 [4096, 4096], P('seq', 'head')
The draws below stay inside these ranges and needn't reach their ends.
Inputs may be any that keep to these rules, and one draw needn't show every extreme that they name: `random_blocks`: for the 4 query blocks of one index of seq, at most 2 of their random entries name blocks of any one index of seq, and exactly 2 name blocks of some index of seq. `global_blocks`: the 2 global blocks are distinct, and one of them, at a position that varies, is the last block of the sequence.
All inputs are finite; a program needn't handle non-finite values.
Results may differ from the reference program's by a relative error of at most 0.04.
Values may be sent and summed in bfloat16 or wider, within the bound.
A program may use at most 192 MiB of HBM per device.

```python
import math
import jax
import jax.numpy as jnp
from jax import lax

D = 4096
H = 32
HD = 128
BLK = 64
RAND = 3
GLOB = 2
TOKENS = 4096
NB = 64
QBD = 4
SHARDS = 16
CAP = 2


def query_key_pair(key):
    base = jax.random.fold_in(key, 17)
    first, second = jax.random.split(base, 2)
    query_vals = jnp.clip(jax.random.normal(first, (TOKENS, D), jnp.float32), -4.0, 4.0)
    key_vals = jnp.clip(jax.random.normal(second, (TOKENS, D), jnp.float32), -4.0, 4.0)
    columns = jnp.exp(jnp.log(3.0) * jnp.arange(D, dtype=jnp.float32) / D)
    query_vals = query_vals * columns[None, :]
    key_vals = key_vals * columns[None, :]
    return (query_vals, key_vals)


def draw_query_in(key, part):
    return query_key_pair(key)[0].astype(jnp.bfloat16)


def draw_key_in(key, part):
    return query_key_pair(key)[1].astype(jnp.bfloat16)


def draw_random_blocks(key, part):
    slot_count = RAND * QBD
    shard_keys = jax.random.split(jax.random.fold_in(key, 3), SHARDS)

    def one_shard(shard_key):
        key_hot, key_perm, key_place = jax.random.split(shard_key, 3)
        hottest = jax.random.randint(key_hot, (), 0, SHARDS)
        slot_ids = jnp.arange(slot_count)
        others = (hottest + 1 + (slot_ids - CAP) % (SHARDS - 1)) % SHARDS
        owners = jnp.where(slot_ids < CAP, hottest, others)
        owners = owners[jax.random.permutation(key_perm, slot_count)]
        places = jax.random.randint(key_place, (slot_count,), 0, QBD)
        return (owners * QBD + places).reshape(QBD, RAND)
    return jax.vmap(one_shard)(shard_keys).reshape(NB, RAND).astype(jnp.int32)


def draw_global_blocks(key, part):
    base = jax.random.fold_in(key, 5)
    key_pick, key_order = jax.random.split(base, 2)
    picked = jax.random.permutation(key_pick, NB - 1)[:GLOB - 1].astype(jnp.int32)
    chosen = jnp.concatenate([picked, jnp.full((1,), NB - 1, jnp.int32)])
    return chosen[jax.random.permutation(key_order, GLOB)].astype(jnp.int32)


def steps_of(rng, shape, pieces, smallest, high):
    level, own = 1.0, jax.random.fold_in(rng, 6)
    for position, blocks in pieces:
        heights = jnp.exp(jax.random.uniform(jax.random.fold_in(own, position), (blocks,), jnp.float32, smallest / len(pieces), high / len(pieces)))
        level = level * jnp.repeat(heights, shape[position] // blocks).reshape([-1 if axis == position else 1 for axis in range(len(shape))])
    return level


def normal_values(rng, extent, scale, most, shards=(), kind=jnp.bfloat16):
    array = scale * jax.random.normal(rng, extent, jnp.float32)
    if shards:
        array = array * steps_of(rng, extent, shards, -0.22, 0.18)
    return jnp.clip(array, -most, most).astype(kind)


def setup_inputs(seed: int = 0) -> dict:
    seeds = jax.random.split(jax.random.key(seed), 9)
    query_in = draw_query_in(jax.random.fold_in(seeds[8], 71), 0)
    key_in = draw_key_in(jax.random.fold_in(seeds[8], 71), 0)
    value_in = normal_values(seeds[2], (TOKENS, D), 1.0, 6.0, ((0, 16), (1, 2)))
    out_grad = normal_values(seeds[3], (TOKENS, D), 1.0, 6.0, ((0, 16), (1, 2)))
    query_gain = jnp.clip(jnp.exp(math.log(2.0) - 1.3862944 * jax.random.uniform(seeds[4], (D,), jnp.float32) ** steps_of(seeds[4], (D,), ((0, 2),), -0.2, 0.2)), 0.5, 2.0)
    key_gain = jnp.clip(jnp.exp(math.log(2.0) - 1.3862944 * jax.random.uniform(seeds[5], (D,), jnp.float32) ** steps_of(seeds[5], (D,), ((0, 2),), -0.2, 0.2)), 0.5, 2.0)
    random_blocks = draw_random_blocks(jax.random.fold_in(seeds[8], 71), 0)
    global_blocks = draw_global_blocks(jax.random.fold_in(seeds[8], 71), 0)
    return dict(query_in=query_in, key_in=key_in, value_in=value_in, out_grad=out_grad, query_gain=query_gain, key_gain=key_gain, random_blocks=random_blocks, global_blocks=global_blocks)


EPS = 1e-06
NEG = -1e+30

def normed(values, gain):
    full = values.astype(jnp.float32)
    inverse = lax.rsqrt(lax.optimization_barrier(jnp.sum(full * full, axis=1)) / D + EPS)
    return (full, inverse, (full * inverse[:, None] * gain[None, :]).astype(jnp.bfloat16))

def norm_grad(full, inverse, gain, grad):
    total = lax.optimization_barrier(jnp.sum(full * gain[None, :] * grad, axis=1))
    result = inverse[:, None] * gain[None, :] * grad - full * (inverse ** 3 * total / D)[:, None]
    return result.astype(jnp.bfloat16)

def round_trip(values):
    return lax.optimization_barrier(values.astype(jnp.bfloat16)).astype(jnp.float32)

def reference(query_in, key_in, value_in, out_grad, query_gain, key_gain, random_blocks, global_blocks):
    scale = HD ** (-0.5)
    list_len = 3 + RAND + GLOB
    block_total = TOKENS // BLK
    query_f, query_rms, query_normed = normed(query_in, query_gain)
    key_f, key_rms, key_normed = normed(key_in, key_gain)
    query_blk = query_normed.reshape(block_total, BLK, H, HD)
    key_blk = key_normed.reshape(block_total, BLK, H, HD)
    value_blk = value_in.reshape(block_total, BLK, H, HD)
    grad_blk = out_grad.reshape(block_total, BLK, H, HD)

    def block_step(carry, index):
        key_acc, value_acc = carry
        window_ids = jnp.stack([index - 1, index, index + 1]).astype(jnp.int32)
        list_ids = jnp.concatenate([window_ids, random_blocks[index].astype(jnp.int32), global_blocks.astype(jnp.int32)])
        valid = (list_ids >= 0) & (list_ids < block_total)
        clipped = jnp.clip(list_ids, 0, block_total - 1)
        keys_here = key_blk[clipped].reshape(list_len * BLK, H, HD).astype(jnp.float32)
        values_here = value_blk[clipped].reshape(list_len * BLK, H, HD).astype(jnp.float32)
        query_here = query_blk[index].astype(jnp.float32)
        grad_here = grad_blk[index].astype(jnp.float32)
        key_ok = jnp.repeat(valid, BLK)
        scores = jnp.einsum('qhd,khd->hqk', query_here, keys_here) * scale
        scores = jnp.where(key_ok[None, None, :], scores, NEG)
        top = lax.optimization_barrier(jnp.max(scores, axis=-1, keepdims=True))
        expd = jnp.exp(scores - top)
        prob = expd / lax.optimization_barrier(jnp.sum(expd, axis=-1, keepdims=True))
        prob_bf = round_trip(prob)
        out_block = jnp.einsum('hqk,khd->qhd', prob_bf, values_here).astype(jnp.bfloat16)
        delta = lax.optimization_barrier(jnp.sum(grad_here * out_block.astype(jnp.float32), axis=-1))
        dprob = jnp.einsum('qhd,khd->hqk', grad_here, values_here)
        dscore = prob * (dprob - jnp.transpose(delta)[:, :, None])
        dscore_bf = round_trip(dscore)
        dq_block = jnp.einsum('hqk,khd->qhd', dscore_bf, keys_here) * scale
        key_part = (jnp.einsum('hqk,qhd->khd', dscore_bf, query_here) * scale).reshape(list_len, BLK, H, HD)
        value_part = jnp.einsum('hqk,qhd->khd', prob_bf, grad_here).reshape(list_len, BLK, H, HD)
        key_part = jnp.concatenate([key_part[:3], round_trip(key_part[3:3 + RAND]), key_part[3 + RAND:]])
        value_part = jnp.concatenate([value_part[:3], round_trip(value_part[3:3 + RAND]), value_part[3 + RAND:]])
        key_acc = key_acc.at[clipped].add(key_part)
        value_acc = value_acc.at[clipped].add(value_part)
        return ((key_acc, value_acc), (out_block, dq_block))
    start = (jnp.zeros((block_total, BLK, H, HD), jnp.float32), jnp.zeros((block_total, BLK, H, HD), jnp.float32))
    (key_acc, value_acc), (out_blocks, dq_blocks) = lax.scan(block_step, start, jnp.arange(block_total, dtype=jnp.int32))
    attn_out = out_blocks.reshape(TOKENS, D)
    query_grad = norm_grad(query_f, query_rms, query_gain, dq_blocks.reshape(TOKENS, D))
    key_grad = norm_grad(key_f, key_rms, key_gain, key_acc.reshape(TOKENS, D))
    value_grad = value_acc.reshape(TOKENS, D).astype(jnp.bfloat16)
    return (attn_out, query_grad, key_grad, value_grad)
```

```python
import functools
import math

import jax
import jax.numpy as jnp
from jax import lax
from jax.experimental import pallas as pl
from jax.experimental.pallas import tpu as pltpu
from jax.sharding import PartitionSpec as P

HD = 128
BLK = 64
RAND = 3
GLOB = 2
LIST = 3 + RAND + GLOB
EPS = 1e-06
NEG = -1e30
SCALE = HD ** (-0.5)
UNROLL = 4
VMEM = 56 << 20


def params():
    return pltpu.CompilerParams(vmem_limit_bytes=VMEM)


def pack_kernel(heads, q_ref, k_ref, v_ref, g_ref, qr_ref, kr_ref, qg_ref, kg_ref, out_ref):
    for i in range(heads):
        cols = slice(i * HD, (i + 1) * HD)
        out_ref[i, 0] = (
            q_ref[:, cols].astype(jnp.float32) * qr_ref[...] * qg_ref[:, cols]
        ).astype(jnp.bfloat16)
        out_ref[i, 1] = (
            k_ref[:, cols].astype(jnp.float32) * kr_ref[...] * kg_ref[:, cols]
        ).astype(jnp.bfloat16)
        out_ref[i, 2] = v_ref[:, cols]
        out_ref[i, 3] = g_ref[:, cols]


def dot(a, b, dims):
    return lax.dot_general(a, b, (dims, ((), ())), preferred_element_type=jnp.float32)


def attend_kernel(q_blocks, total, rand_ref, glob_ref, in_ref, out_ref, dk_ref, dv_ref):
    dk_ref[...] = jnp.zeros_like(dk_ref)
    dv_ref[...] = jnp.zeros_like(dv_ref)

    def place(block):
        return block // q_blocks, pl.ds(pl.multiple_of(block % q_blocks * BLK, BLK), BLK)

    def row(block):
        return pl.ds(pl.multiple_of(block * BLK, BLK), BLK)

    column = lax.broadcasted_iota(jnp.int32, (1, LIST * BLK), 1)

    def group(step, carry):
        made = []
        for sub in range(UNROLL):
            b = step * UNROLL + sub
            names = [jnp.maximum(b - 1, 0), b, jnp.minimum(b + 1, total - 1)]
            names += [rand_ref[b * RAND + i] for i in range(RAND)]
            names += [glob_ref[i] for i in range(GLOB)]
            spots = [place(n) for n in names]
            keys = jnp.concatenate([in_ref[s, 1, r, :] for s, r in spots], axis=0)
            values = jnp.concatenate([in_ref[s, 2, r, :] for s, r in spots], axis=0)
            shard, rows = place(b)
            query = in_ref[shard, 0, rows, :]
            grad = in_ref[shard, 3, rows, :]
            low = jnp.where(b == 0, BLK, 0)
            high = jnp.where(b == total - 1, 2 * BLK, 3 * BLK)
            masked = (column < low) | ((column >= high) & (column < 3 * BLK))
            scores = dot(query, keys, ((1,), (1,))) * SCALE
            scores = jnp.where(masked, NEG, scores)
            expd = jnp.exp(scores - jnp.max(scores, axis=1, keepdims=True))
            prob = expd * (1.0 / jnp.sum(expd, axis=1, keepdims=True))
            prob_bf = prob.astype(jnp.bfloat16)
            out = dot(prob_bf, values, ((1,), (0,))).astype(jnp.bfloat16)
            delta = jnp.sum(
                grad.astype(jnp.float32) * out.astype(jnp.float32), axis=1, keepdims=True
            )
            dprob = dot(grad, values, ((1,), (1,)))
            dscore = (prob * (dprob - delta)).astype(jnp.bfloat16)
            dq = dot(dscore, keys, ((1,), (0,))) * SCALE
            dk = dot(dscore, query, ((0,), (0,)))
            dv = dot(prob_bf, grad, ((0,), (0,)))
            made.append((names, shard, rows, out, dq, dk, dv))
        for names, shard, rows, out, dq, dk, dv in made:
            out_ref[shard, 0, rows, :] = out
            out_ref[shard, 1, rows, :] = dq.astype(jnp.bfloat16)
            for i, name in enumerate(names):
                part = slice(i * BLK, (i + 1) * BLK)
                dk_ref[row(name), :] += dk[part]
                dv_ref[row(name), :] += dv[part]
        return carry

    lax.fori_loop(0, total // UNROLL, group, 0)
    tok = q_blocks * BLK
    for shard in range(total // q_blocks):
        rows = slice(shard * tok, (shard + 1) * tok)
        out_ref[shard, 2] = (dk_ref[rows, :] * SCALE).astype(jnp.bfloat16)
        out_ref[shard, 3] = dv_ref[rows, :].astype(jnp.bfloat16)


def sums_kernel(heads, back_ref, q_ref, k_ref, qg_ref, kg_ref, sq_ref, sk_ref):
    @pl.when(pl.program_id(0) == 0)
    def _():
        sq_ref[...] = jnp.zeros_like(sq_ref)
        sk_ref[...] = jnp.zeros_like(sk_ref)

    dot_q = jnp.zeros((q_ref.shape[0], HD), jnp.float32)
    dot_k = jnp.zeros((q_ref.shape[0], HD), jnp.float32)
    for i in range(heads):
        cols = slice(i * HD, (i + 1) * HD)
        dot_q += q_ref[:, cols].astype(jnp.float32) * qg_ref[:, cols] * back_ref[i, 1].astype(jnp.float32)
        dot_k += k_ref[:, cols].astype(jnp.float32) * kg_ref[:, cols] * back_ref[i, 2].astype(jnp.float32)
    sq_ref[...] += jnp.sum(dot_q, axis=1, keepdims=True)
    sk_ref[...] += jnp.sum(dot_k, axis=1, keepdims=True)


def finish_kernel(
    heads, back_ref, q_ref, k_ref, qg_ref, kg_ref, qr_ref, kr_ref, qt_ref, kt_ref,
    out_ref, dq_ref, dk_ref, dv_ref,
):
    for i in range(heads):
        cols = slice(i * HD, (i + 1) * HD)
        out_ref[:, cols] = back_ref[i, 0]
        dv_ref[:, cols] = back_ref[i, 3]
        dq_ref[:, cols] = (
            qr_ref[...] * qg_ref[:, cols] * back_ref[i, 1].astype(jnp.float32)
            - q_ref[:, cols].astype(jnp.float32) * qt_ref[...]
        ).astype(jnp.bfloat16)
        dk_ref[:, cols] = (
            kr_ref[...] * kg_ref[:, cols] * back_ref[i, 2].astype(jnp.float32)
            - k_ref[:, cols].astype(jnp.float32) * kt_ref[...]
        ).astype(jnp.bfloat16)


def shards(
    query_in, key_in, value_in, out_grad, query_gain, key_gain, random_blocks, global_blocks
):
    tok, feats = query_in.shape
    heads = feats // HD
    width = feats * lax.axis_size("head")
    seq = lax.axis_size("seq")
    q_blocks = tok // BLK
    total = q_blocks * seq
    copies = seq // heads
    per = math.gcd(heads, 4)
    steps = heads // per
    shape = jax.ShapeDtypeStruct

    token_spec = pl.BlockSpec((tok, per * HD), lambda i: (0, i))
    gain_spec = pl.BlockSpec((1, per * HD), lambda i: (0, i))
    row_spec = pl.BlockSpec((tok, 1), lambda i: (0, 0))
    head_spec = pl.BlockSpec((per, 4, tok, HD), lambda i: (i, 0, 0, 0))

    query_f = query_in.astype(jnp.float32)
    key_f = key_in.astype(jnp.float32)
    sums = jnp.stack([jnp.sum(query_f * query_f, axis=1), jnp.sum(key_f * key_f, axis=1)])
    sums = lax.psum(sums, "head")
    rms = lax.rsqrt(sums / width + EPS)
    query_rms, key_rms = rms[0][:, None], rms[1][:, None]
    query_gain, key_gain = query_gain[None], key_gain[None]

    packed = pl.pallas_call(
        functools.partial(pack_kernel, per),
        grid=(steps,),
        in_specs=[token_spec] * 4 + [row_spec] * 2 + [gain_spec] * 2,
        out_specs=head_spec,
        out_shape=shape((heads, 4, tok, HD), jnp.bfloat16),
        compiler_params=params(),
        name="pack",
    )(query_in, key_in, value_in, out_grad, query_rms, key_rms, query_gain, key_gain)
    if copies > 1:
        packed = jnp.repeat(packed, copies, axis=0)
    arrived = lax.all_to_all(packed, "seq", split_axis=0, concat_axis=0, tiled=True)
    result = pl.pallas_call(
        functools.partial(attend_kernel, q_blocks, total),
        in_specs=[pl.BlockSpec(memory_space=pltpu.SMEM)] * 2
        + [pl.BlockSpec(memory_space=pltpu.VMEM)],
        out_specs=pl.BlockSpec(memory_space=pltpu.VMEM),
        out_shape=shape((seq, 4, tok, HD), jnp.bfloat16),
        scratch_shapes=[pltpu.VMEM((tok * seq, HD), jnp.float32)] * 2,
        compiler_params=params(),
        name="attend",
    )(random_blocks.reshape(-1), global_blocks, arrived)
    back = lax.all_to_all(result, "seq", split_axis=0, concat_axis=0, tiled=True)
    if copies > 1:
        back = back[::copies]
    totals = pl.pallas_call(
        functools.partial(sums_kernel, per),
        grid=(steps,),
        in_specs=[head_spec] + [token_spec] * 2 + [gain_spec] * 2,
        out_specs=[row_spec] * 2,
        out_shape=[shape((tok, 1), jnp.float32)] * 2,
        compiler_params=params(),
        name="sums",
    )(back, query_in, key_in, query_gain, key_gain)
    total_query, total_key = lax.psum(tuple(totals), "head")
    query_term = query_rms**3 * total_query / width
    key_term = key_rms**3 * total_key / width
    return tuple(
        pl.pallas_call(
            functools.partial(finish_kernel, per),
            grid=(steps,),
            in_specs=[head_spec] + [token_spec] * 2 + [gain_spec] * 2 + [row_spec] * 4,
            out_specs=[token_spec] * 4,
            out_shape=[shape((tok, feats), jnp.bfloat16)] * 4,
            compiler_params=params(),
            name="finish",
        )(back, query_in, key_in, query_gain, key_gain, query_rms, key_rms, query_term, key_term)
    )


def solution(mesh):
    token = P("seq", "head")
    in_specs = (token,) * 4 + (P("head"),) * 2 + (P(),) * 2
    return jax.shard_map(
        shards, mesh=mesh, in_specs=in_specs, out_specs=(token,) * 4, check_vma=False
    )
```
